32 devices in a mesh: row: 8 (over z, x), col: 4 (over y, core).
Axes of the slice: x: 2, y: 2, z: 4, core: 2. Of those that a mesh axis runs over, the one named last changes fastest.
Arguments:
- tokens: bfloat16 [4096, 4096], P('row', 'col'), may hold values from -6 to 6
- gate_weight: bfloat16 [4096, 16384], P('row', 'col'), may hold values from -0.125 to 0.125
- up_weight: bfloat16 [4096, 16384], P('row', 'col'), may hold values from -0.125 to 0.125
- tile_mask: int32 [32, 128], P(None, 'col'), may hold values from 0 to 1, as said below
Outputs:
- hidden: bfloat16 [4096, 16384], P('row', 'col')
The draws below stay inside these ranges and needn't reach their ends.
Inputs may be any that keep to these rules, and one draw needn't show every extreme that they name: `tile_mask`: values are 0 or 1. In each aligned block of 4 x 32 tiles (tile rows r * 4 to (r + 1) * 4 - 1, tile columns c * 32 to (c + 1) * 32 - 1) at least 48 and at most 80 tiles are kept; some block keeps exactly 80.
All inputs are finite; a program needn't handle non-finite values.
Results may differ from the reference program's by a relative error of at most 0.001.
Values may be sent and summed in bfloat16 or wider, within the bound.
A program may use at most 128 MiB of HBM per device.

```python
import jax
import jax.numpy as jnp

D = 4096
F = 16384
TILE = 128
TOKENS = 4096
RB = 4
CB = 32
KEEP_MOST = 80
N_ROW = 8
N_COL = 4


def draw_tile_mask(key, part):
    key_count, key_chosen, key_score = jax.random.split(key, 3)
    tile_count = RB * CB
    fewest = 3 * tile_count // 8
    blocks = N_ROW * N_COL
    counts = jax.random.randint(key_count, (blocks,), fewest, KEEP_MOST + 1)
    chosen = jax.random.randint(key_chosen, (), 0, blocks)
    counts = jnp.where(jnp.arange(blocks) == chosen, KEEP_MOST, counts)
    scores = jax.random.randint(key_score, (blocks, tile_count), 0, 65536) * tile_count + jnp.arange(tile_count)[None, :]
    ordering = jnp.argsort(scores, axis=1, stable=True)
    ranking = jnp.argsort(ordering, axis=1, stable=True)
    kept_tiles = (ranking < counts[:, None]).astype(jnp.int32)
    kept_tiles = kept_tiles.reshape(N_ROW, N_COL, RB, CB).transpose(0, 2, 1, 3)
    return kept_tiles.reshape(N_ROW * RB, N_COL * CB)


def level_of(key, dims, cuts, low, largest):
    factor_of, own = 1.0, jax.random.fold_in(key, 6)
    for position, shards_of in cuts:
        steps = jnp.exp(jax.random.uniform(jax.random.fold_in(own, position), (shards_of,), jnp.float32, low / len(cuts), largest / len(cuts)))
        factor_of = factor_of * jnp.repeat(steps, dims[position] // shards_of).reshape([-1 if axis == position else 1 for axis in range(len(dims))])
    return factor_of


def gaussian(own_key, dims, deviation, most, shards=(), kind=jnp.bfloat16):
    factor_of = level_of(own_key, dims, shards, -0.22, 0.18) if shards else 1.0
    drawn = jax.random.normal(own_key, dims, jnp.float32) * deviation * factor_of
    return jnp.minimum(jnp.maximum(drawn, -most), most).astype(kind)


def setup_inputs(seed: int = 0) -> dict:
    key_of = jax.random.split(jax.random.key(seed), 5)
    tokens = gaussian(key_of[0], (TOKENS, D), 1.0, 6.0, ((0, 8), (1, 4)))
    gate_weight = gaussian(key_of[1], (D, F), (D // 2) ** -0.5, 0.125, ((0, 8), (1, 4)))
    up_weight = gaussian(key_of[2], (D, F), (D // 2) ** -0.5, 0.125, ((0, 8), (1, 4)))
    tile_mask = draw_tile_mask(jax.random.fold_in(key_of[4], 71), 0)
    return dict(tokens=tokens, gate_weight=gate_weight, up_weight=up_weight, tile_mask=tile_mask)


def spread_mask(tile_mask, dtype):
    return jnp.repeat(jnp.repeat(tile_mask, TILE, axis=0), TILE, axis=1).astype(dtype)


def reference(tokens, gate_weight, up_weight, tile_mask):
    keep_cells = spread_mask(tile_mask, gate_weight.dtype)
    gate_sum = jnp.dot(tokens, gate_weight * keep_cells, preferred_element_type=jnp.float32)
    up_sum = jnp.dot(tokens, up_weight * keep_cells, preferred_element_type=jnp.float32)
    return (jax.nn.silu(gate_sum) * up_sum).astype(jnp.bfloat16)
```

```python
import functools

import jax
import jax.numpy as jnp
from jax import lax
from jax.experimental import pallas as pl
from jax.experimental.pallas import tpu as pltpu
from jax.sharding import PartitionSpec as P

TILE = 128
VMEM_LIMIT = 56 * 1024 * 1024


def pack_kernel(row_tiles, col_tiles, core_ref, mask_ref, gate_ref, up_ref, mine_ref, other_ref):
    core = core_ref[0]

    def tile_step(i, j, slot):
        kept = mask_ref[i * col_tiles + j]
        rows = pl.ds(i * TILE, TILE)
        cols = pl.ds(pl.multiple_of(j * TILE, TILE), TILE)

        @pl.when((kept == 1) & (core == 0))
        def _():
            mine_ref[slot] = gate_ref[rows, cols]
            other_ref[slot] = up_ref[rows, cols]

        @pl.when((kept == 1) & (core == 1))
        def _():
            mine_ref[slot] = up_ref[rows, cols]
            other_ref[slot] = gate_ref[rows, cols]

        return slot + kept

    slot = jnp.int32(0)
    for i in range(row_tiles):
        slot = lax.fori_loop(0, col_tiles, functools.partial(tile_step, i), slot)


def block_kernel(row_tiles, col_tiles, chunk_tiles, first, last,
                 codes_ref, info_ref, tok_ref, mine_ref, other_ref, *rest):
    if first:
        acc_ref = None
        out_ref, dense = rest
    else:
        acc_ref, out_ref, dense = rest
    block, core = info_ref[0], info_ref[1]
    chunk = pl.program_id(0)
    sums = []
    for kind, packed in enumerate((mine_ref, other_ref)):
        for i in range(row_tiles):
            for j in range(chunk_tiles):
                code = codes_ref[(block * row_tiles + i) * col_tiles + chunk * chunk_tiles + j]
                tile = packed[jnp.maximum(code, 0)]
                dense[kind, pl.ds(i * TILE, TILE), pl.ds(j * TILE, TILE)] = jnp.where(
                    code >= 0, tile, jnp.zeros_like(tile))
        total = jnp.dot(tok_ref[...], dense[kind], preferred_element_type=jnp.float32)
        if not first:
            total = total + acc_ref[kind]
        if last:
            sums.append(total)
        else:
            out_ref[kind] = total
    if last:
        gate = jnp.where(core == 0, sums[0], sums[1])
        up = jnp.where(core == 0, sums[1], sums[0])
        out_ref[...] = (gate / (1.0 + jnp.exp(-gate)) * up).astype(out_ref.dtype)


def solution(mesh):
    R, C = mesh.shape["row"], mesh.shape["col"]
    NZ = R // 2
    axes = ("row", "col")

    def send(value, move):
        pairs = []
        for r in range(R):
            for c in range(C):
                tr, tc = move(r, c)
                pairs.append((r * C + c, tr * C + tc))
        return lax.ppermute(value, axes, pairs)

    sibling = lambda r, c: (r, c ^ 1)
    z_pair = lambda r, c: (r ^ 2, c)
    x_pair = lambda r, c: (r ^ 1, c)

    def swap_out(r, c):
        return (r, c) if ((r // 2) % 2) == (c % 2) else (r ^ 2, c ^ 1)

    def on_device(tokens, gate_weight, up_weight, tile_mask):
        depth, cols = gate_weight.shape
        row_tiles, col_tiles = depth // TILE, cols // TILE
        slots = 5 * row_tiles * col_tiles // 8
        rows = tokens.shape[0]
        r = lax.axis_index("row")
        core = lax.axis_index("col") % 2
        home = ((r // 2) % 2) == core

        smem = pl.BlockSpec(memory_space=pltpu.SMEM)
        vmem = pl.BlockSpec(memory_space=pltpu.VMEM)
        own_mask = lax.dynamic_slice_in_dim(tile_mask, r * row_tiles, row_tiles, 0).reshape(-1)
        piece = jax.ShapeDtypeStruct((slots, TILE, TILE), gate_weight.dtype)
        mine, other = pl.pallas_call(
            functools.partial(pack_kernel, row_tiles, col_tiles),
            out_shape=(piece, piece),
            in_specs=[smem, smem, vmem, vmem],
            out_specs=(vmem, vmem),
            compiler_params=pltpu.CompilerParams(vmem_limit_bytes=VMEM_LIMIT),
            name="pack",
        )(core.reshape(1).astype(jnp.int32), own_mask, gate_weight, up_weight)

        tok_other = send(tokens, z_pair)
        tok_mine = jnp.where(home, tokens, tok_other)
        tok_sib = send(jnp.where(home, tok_other, tokens), sibling)
        wide = tokens.shape[1]
        both = jnp.where(core == 0, jnp.concatenate([tok_mine, tok_sib], 1),
                         jnp.concatenate([tok_sib, tok_mine], 1))
        y = lax.axis_index("col") // 2
        tok = jnp.zeros((rows, wide * C), tokens.dtype)
        tok = lax.dynamic_update_slice_in_dim(tok, both, y * 2 * wide, 1)
        for s in range(1, C // 2):
            part = send(both, lambda rr, cc, s=s: (rr, (cc + 2 * s) % C))
            source = (y - s) % (C // 2)
            tok = lax.dynamic_update_slice_in_dim(tok, part, source * 2 * wide, 1)

        mask_sib = send(tile_mask, sibling)
        job_mask = jnp.where(home, tile_mask, mask_sib).reshape(R, row_tiles * col_tiles)
        place = jnp.arange(row_tiles * col_tiles)
        upto = (place[None, :] <= place[:, None]).astype(jnp.int32)
        slot = jnp.sum(job_mask[:, None, :] * upto[None], axis=2) - 1
        codes = jnp.where(job_mask == 1, slot, -1).reshape(-1)

        crossed = send(other, sibling)
        keep = jnp.where(home, mine, crossed)
        give = jnp.where(home, crossed, mine)
        own = [(keep, r), (send(give, z_pair), r ^ 2)]
        pieces = []
        for value, block in own:
            pieces.append((value, block))
            for s in range(1, NZ // 2):
                moved = send(value, lambda rr, cc, s=s: ((rr + 4 * s) % R, cc))
                pieces.append((moved, (block - 4 * s) % R))
        order = []
        for value, block in pieces:
            order.append((value, block))
            order.append((send(value, x_pair), block ^ 1))

        chunk_tiles = min(4, col_tiles)
        width = chunk_tiles * TILE
        acc = None
        for n, (value, block) in enumerate(order):
            across = send(value, sibling)
            first, last = n == 0, n == len(order) - 1
            info = jnp.stack([block, core]).astype(jnp.int32)
            whole = pl.BlockSpec((slots, TILE, TILE), lambda g, *_: (0, 0, 0))
            acc_spec = pl.BlockSpec((2, rows, width), lambda g, *_: (0, 0, g))
            in_specs = [pl.BlockSpec((rows, depth), lambda g, codes, info: (0, info[0])), whole, whole]
            operands = [codes, info, tok, value, across]
            if not first:
                in_specs.append(acc_spec)
                operands.append(acc)
            if last:
                out_shape = jax.ShapeDtypeStruct((rows, cols), jnp.bfloat16)
                out_spec = pl.BlockSpec((rows, width), lambda g, *_: (0, g))
            else:
                out_shape = jax.ShapeDtypeStruct((2, rows, cols), jnp.float32)
                out_spec = acc_spec
            acc = pl.pallas_call(
                functools.partial(block_kernel, row_tiles, col_tiles, chunk_tiles, first, last),
                out_shape=out_shape,
                grid_spec=pltpu.PrefetchScalarGridSpec(
                    num_scalar_prefetch=2,
                    grid=(cols // width,),
                    in_specs=in_specs,
                    out_specs=out_spec,
                    scratch_shapes=[pltpu.VMEM((2, depth, width), jnp.bfloat16)],
                ),
                input_output_aliases={} if first or last else {5: 0},
                compiler_params=pltpu.CompilerParams(vmem_limit_bytes=VMEM_LIMIT),
                cost_estimate=pl.CostEstimate(
                    flops=4 * rows * depth * cols,
                    bytes_accessed=8 * rows * cols * 2 + 4 * slots * TILE * TILE,
                    transcendentals=0),
                name="block",
            )(*operands)
        return send(acc, swap_out)

    placed = (P("row", "col"), P("row", "col"), P("row", "col"), P(None, "col"))
    return jax.shard_map(
        on_device, mesh=mesh, in_specs=placed, out_specs=P("row", "col"), check_vma=False
    )
```

```python
import functools

import jax
import jax.numpy as jnp
from jax import lax
from jax.experimental import pallas as pl
from jax.experimental.pallas import tpu as pltpu
from jax.sharding import PartitionSpec as P

TILE = 128
VMEM_LIMIT = 56 * 1024 * 1024


def pack_kernel(row_tiles, col_tiles, core_ref, mask_ref, gate_ref, up_ref, mine_ref, other_ref):
    core = core_ref[0]

    def tile_step(i, j, slot):
        kept = mask_ref[i * col_tiles + j]
        rows = pl.ds(i * TILE, TILE)
        cols = pl.ds(pl.multiple_of(j * TILE, TILE), TILE)

        @pl.when((kept == 1) & (core == 0))
        def _():
            mine_ref[slot] = gate_ref[rows, cols]
            other_ref[slot] = up_ref[rows, cols]

        @pl.when((kept == 1) & (core == 1))
        def _():
            mine_ref[slot] = up_ref[rows, cols]
            other_ref[slot] = gate_ref[rows, cols]

        return slot + kept

    slot = jnp.int32(0)
    for i in range(row_tiles):
        slot = lax.fori_loop(0, col_tiles, functools.partial(tile_step, i), slot)


def block_kernel(row_tiles, col_tiles, chunk_tiles, parts, first, last,
                 codes_ref, info_ref, tok_ref, *rest):
    pieces, rest = rest[:2 * parts], rest[2 * parts:]
    if first:
        acc_ref = None
    else:
        acc_ref, rest = rest[0], rest[1:]
    out_ref, packed, dense, sems = rest
    block, core = info_ref[0], info_ref[1]
    chunk = pl.program_id(0)

    @pl.when(chunk == 0)
    def _():
        copies = []
        for kind in range(2):
            start = 0
            for n in range(parts):
                ref = pieces[kind * parts + n]
                count = ref.shape[0]
                copies.append(pltpu.make_async_copy(
                    ref, packed.at[kind, pl.ds(start, count)], sems.at[kind, n]))
                start += count
        for copy in copies:
            copy.start()
        for copy in copies:
            copy.wait()

    sums = []
    for kind in range(2):
        for i in range(row_tiles):
            for j in range(chunk_tiles):
                code = codes_ref[(block * row_tiles + i) * col_tiles + chunk * chunk_tiles + j]
                tile = packed[kind, jnp.maximum(code, 0)]
                dense[kind, pl.ds(i * TILE, TILE), pl.ds(j * TILE, TILE)] = jnp.where(
                    code >= 0, tile, jnp.zeros_like(tile))
        total = jnp.dot(tok_ref[...], dense[kind], preferred_element_type=jnp.float32)
        if not first:
            total = total + acc_ref[kind]
        if last:
            sums.append(total)
        else:
            out_ref[kind] = total
    if last:
        gate = jnp.where(core == 0, sums[0], sums[1])
        up = jnp.where(core == 0, sums[1], sums[0])
        out_ref[...] = (gate / (1.0 + jnp.exp(-gate)) * up).astype(out_ref.dtype)


def solution(mesh):
    R, C = mesh.shape["row"], mesh.shape["col"]
    NZ = R // 2
    axes = ("row", "col")

    def send(value, move):
        pairs = []
        for r in range(R):
            for c in range(C):
                tr, tc = move(r, c)
                pairs.append((r * C + c, tr * C + tc))
        return lax.ppermute(value, axes, pairs)

    sibling = lambda r, c: (r, c ^ 1)
    z_pair = lambda r, c: (r ^ 2, c)
    x_pair = lambda r, c: (r ^ 1, c)

    def swap_out(r, c):
        return (r, c) if ((r // 2) % 2) == (c % 2) else (r ^ 2, c ^ 1)

    def on_device(tokens, gate_weight, up_weight, tile_mask):
        depth, cols = gate_weight.shape
        row_tiles, col_tiles = depth // TILE, cols // TILE
        slots = 5 * row_tiles * col_tiles // 8
        rows = tokens.shape[0]
        r = lax.axis_index("row")
        core = lax.axis_index("col") % 2
        home = ((r // 2) % 2) == core

        smem = pl.BlockSpec(memory_space=pltpu.SMEM)
        vmem = pl.BlockSpec(memory_space=pltpu.VMEM)
        own_mask = lax.dynamic_slice_in_dim(tile_mask, r * row_tiles, row_tiles, 0).reshape(-1)
        piece = jax.ShapeDtypeStruct((slots, TILE, TILE), gate_weight.dtype)
        mine, other = pl.pallas_call(
            functools.partial(pack_kernel, row_tiles, col_tiles),
            out_shape=(piece, piece),
            in_specs=[smem, smem, vmem, vmem],
            out_specs=(vmem, vmem),
            compiler_params=pltpu.CompilerParams(vmem_limit_bytes=VMEM_LIMIT),
            name="pack",
        )(core.reshape(1).astype(jnp.int32), own_mask, gate_weight, up_weight)

        mask_sib = send(tile_mask, sibling)
        job_mask = jnp.where(home, tile_mask, mask_sib).reshape(R, row_tiles * col_tiles)
        place = jnp.arange(row_tiles * col_tiles)
        upto = (place[None, :] <= place[:, None]).astype(jnp.int32)
        slot = jnp.sum(job_mask[:, None, :] * upto[None], axis=2) - 1
        codes = jnp.where(job_mask == 1, slot, -1).reshape(-1)

        crossed = send(other, sibling)
        keep = jnp.where(home, mine, crossed)
        give = jnp.where(home, crossed, mine)
        chunk_tiles = min(4, col_tiles)
        width = chunk_tiles * TILE

        def add_block(acc, values, block, last=False):
            first, parts = acc is None, len(values)
            info = jnp.stack([block, core]).astype(jnp.int32)
            acc_spec = pl.BlockSpec((2, rows, width), lambda g, *_: (0, 0, g))
            in_specs = [pl.BlockSpec((rows, depth), lambda g, codes, info: (0, info[0]))]
            in_specs += [pl.BlockSpec(memory_space=pl.ANY)] * (2 * parts)
            operands = [codes, info, tok] + [v for v, _ in values] + [w for _, w in values]
            if not first:
                in_specs.append(acc_spec)
                operands.append(acc)
            if last:
                out_shape = jax.ShapeDtypeStruct((rows, cols), jnp.bfloat16)
                out_spec = pl.BlockSpec((rows, width), lambda g, *_: (0, g))
            else:
                out_shape = jax.ShapeDtypeStruct((2, rows, cols), jnp.float32)
                out_spec = acc_spec
            return pl.pallas_call(
                functools.partial(block_kernel, row_tiles, col_tiles, chunk_tiles, parts, first, last),
                out_shape=out_shape,
                grid_spec=pltpu.PrefetchScalarGridSpec(
                    num_scalar_prefetch=2,
                    grid=(cols // width,),
                    in_specs=in_specs,
                    out_specs=out_spec,
                    scratch_shapes=[pltpu.VMEM((2, slots, TILE, TILE), jnp.bfloat16),
                                    pltpu.VMEM((2, depth, width), jnp.bfloat16),
                                    pltpu.SemaphoreType.DMA((2, parts))],
                ),
                input_output_aliases={} if first or last else {len(operands) - 1: 0},
                compiler_params=pltpu.CompilerParams(vmem_limit_bytes=VMEM_LIMIT),
                cost_estimate=pl.CostEstimate(
                    flops=rows * depth,
                    bytes_accessed=rows * depth,
                    transcendentals=0),
                name="block",
            )(*operands)

        def after(value, acc):
            return lax.optimization_barrier((value, acc))

        def along(value, s):
            return send(value, lambda rr, cc: ((rr + 4 * s) % R, cc))

        def with_sibling(value):
            return (value, send(value, sibling))

        paired = send(give, z_pair)
        far = [along(keep, s) for s in range(1, NZ // 2)]
        keep_x = send(keep, x_pair)
        tok_other = send(tokens, z_pair)
        half = slots // 2
        far, paired = after(far, paired)
        far_paired = [along(paired, s) for s in range(1, NZ // 2)]
        far_x = [send(value, x_pair) for value in far]
        paired_x = send(paired, x_pair)
        tok_other, (far, keep_x) = after(tok_other, (far, keep_x))
        tok_mine = jnp.where(home, tokens, tok_other)
        tok_sib = send(jnp.where(home, tok_other, tokens), sibling)
        wide = tokens.shape[1]
        both = jnp.where(core == 0, jnp.concatenate([tok_mine, tok_sib], 1),
                         jnp.concatenate([tok_sib, tok_mine], 1))
        y = lax.axis_index("col") // 2
        tok = jnp.zeros((rows, wide * C), tokens.dtype)
        tok = lax.dynamic_update_slice_in_dim(tok, both, y * 2 * wide, 1)
        for s in range(1, C // 2):
            part = send(both, lambda rr, cc, s=s: (rr, (cc + 2 * s) % C))
            source = (y - s) % (C // 2)
            tok = lax.dynamic_update_slice_in_dim(tok, part, source * 2 * wide, 1)

        acc = add_block(None, [with_sibling(keep)], r)
        acc = add_block(acc, [with_sibling(keep_x)], r ^ 1)
        acc = add_block(acc, [with_sibling(paired)], r ^ 2)
        for s, value in enumerate(far, 1):
            acc = add_block(acc, [with_sibling(value)], (r - 4 * s) % R)
        far_paired, acc = after(far_paired, acc)
        (far_x, paired_x), far_paired = after((far_x, paired_x), far_paired)
        last_a = [send(value[:half], x_pair) for value in far_paired]
        last_b = [along(paired_x[half:], s) for s in range(1, NZ // 2)]
        for s, value in enumerate(far_x, 1):
            acc = add_block(acc, [with_sibling(value)], ((r - 4 * s) % R) ^ 1)
        acc = add_block(acc, [with_sibling(paired_x)], r ^ 3)
        for s, value in enumerate(far_paired, 1):
            acc = add_block(acc, [with_sibling(value)], ((r ^ 2) - 4 * s) % R)
        (last_a, last_b), acc = after((last_a, last_b), acc)
        for s in range(1, NZ // 2):
            acc = add_block(acc, [with_sibling(last_a[s - 1]), with_sibling(last_b[s - 1])],
                            (((r ^ 2) - 4 * s) % R) ^ 1, last=s == NZ // 2 - 1)
        return send(acc, swap_out)

    placed = (P("row", "col"), P("row", "col"), P("row", "col"), P(None, "col"))
    return jax.shard_map(
        on_device, mesh=mesh, in_specs=placed, out_specs=P("row", "col"), check_vma=False
    )
```

```python
import functools

import jax
import jax.numpy as jnp
from jax import lax
from jax.experimental import pallas as pl
from jax.experimental.pallas import tpu as pltpu
from jax.sharding import PartitionSpec as P

TILE = 128
VMEM_LIMIT = 56 * 1024 * 1024


def pack_kernel(row_tiles, col_tiles, core_ref, mask_ref, gate_ref, up_ref, mine_ref, other_ref):
    core = core_ref[0]

    def tile_step(i, j, slot):
        kept = mask_ref[i * col_tiles + j]
        rows = pl.ds(i * TILE, TILE)
        cols = pl.ds(pl.multiple_of(j * TILE, TILE), TILE)

        @pl.when((kept == 1) & (core == 0))
        def _():
            mine_ref[slot] = gate_ref[rows, cols]
            other_ref[slot] = up_ref[rows, cols]

        @pl.when((kept == 1) & (core == 1))
        def _():
            mine_ref[slot] = up_ref[rows, cols]
            other_ref[slot] = gate_ref[rows, cols]

        return slot + kept

    slot = jnp.int32(0)
    for i in range(row_tiles):
        slot = lax.fori_loop(0, col_tiles, functools.partial(tile_step, i), slot)


def block_kernel(row_tiles, col_tiles, chunk_tiles, counts, first, last, codes_ref, info_ref, *rest):
    blocks = len(counts)
    tok_refs, rest = rest[:blocks], rest[blocks:]
    pieces, rest = rest[:2 * sum(counts)], rest[2 * sum(counts):]
    if first:
        acc_ref = None
    else:
        acc_ref, rest = rest[0], rest[1:]
    out_ref, packed, dense, sems = rest
    core = info_ref[blocks]
    chunk = pl.program_id(0)

    @pl.when(chunk == 0)
    def _():
        copies = []
        for b in range(blocks):
            for kind in range(2):
                start = 0
                for _ in range(counts[b]):
                    ref = pieces[len(copies)]
                    copies.append(pltpu.make_async_copy(
                        ref, packed.at[b, kind, pl.ds(start, ref.shape[0])], sems.at[len(copies)]))
                    start += ref.shape[0]
        for copy in copies:
            copy.start()
        for copy in copies:
            copy.wait()

    sums = []
    for kind in range(2):
        total = None if first else acc_ref[kind]
        for b in range(blocks):
            for i in range(row_tiles):
                for j in range(chunk_tiles):
                    code = codes_ref[(info_ref[b] * row_tiles + i) * col_tiles + chunk * chunk_tiles + j]
                    tile = packed[b, kind, jnp.maximum(code, 0)]
                    dense[b, kind, pl.ds(i * TILE, TILE), pl.ds(j * TILE, TILE)] = jnp.where(
                        code >= 0, tile, jnp.zeros_like(tile))
            product = jnp.dot(tok_refs[b][...], dense[b, kind], preferred_element_type=jnp.float32)
            total = product if total is None else total + product
        if last:
            sums.append(total)
        else:
            out_ref[kind] = total
    if last:
        gate = jnp.where(core == 0, sums[0], sums[1])
        up = jnp.where(core == 0, sums[1], sums[0])
        out_ref[...] = (gate / (1.0 + jnp.exp(-gate)) * up).astype(out_ref.dtype)


def solution(mesh):
    R, C = mesh.shape["row"], mesh.shape["col"]
    NZ = R // 2
    axes = ("row", "col")

    def send(value, move):
        pairs = []
        for r in range(R):
            for c in range(C):
                tr, tc = move(r, c)
                pairs.append((r * C + c, tr * C + tc))
        return lax.ppermute(value, axes, pairs)

    sibling = lambda r, c: (r, c ^ 1)
    z_pair = lambda r, c: (r ^ 2, c)
    x_pair = lambda r, c: (r ^ 1, c)

    def swap_out(r, c):
        return (r, c) if ((r // 2) % 2) == (c % 2) else (r ^ 2, c ^ 1)

    def on_device(tokens, gate_weight, up_weight, tile_mask):
        depth, cols = gate_weight.shape
        row_tiles, col_tiles = depth // TILE, cols // TILE
        slots = 5 * row_tiles * col_tiles // 8
        rows = tokens.shape[0]
        r = lax.axis_index("row")
        core = lax.axis_index("col") % 2
        home = ((r // 2) % 2) == core

        def after(value, acc):
            return lax.optimization_barrier((value, acc))

        tok_other = send(tokens, z_pair)
        smem = pl.BlockSpec(memory_space=pltpu.SMEM)
        vmem = pl.BlockSpec(memory_space=pltpu.VMEM)
        own_mask = lax.dynamic_slice_in_dim(tile_mask, r * row_tiles, row_tiles, 0).reshape(-1)
        piece = jax.ShapeDtypeStruct((slots, TILE, TILE), gate_weight.dtype)
        mine, other = pl.pallas_call(
            functools.partial(pack_kernel, row_tiles, col_tiles),
            out_shape=(piece, piece),
            in_specs=[smem, smem, vmem, vmem],
            out_specs=(vmem, vmem),
            compiler_params=pltpu.CompilerParams(vmem_limit_bytes=VMEM_LIMIT),
            name="pack",
        )(core.reshape(1).astype(jnp.int32), own_mask, gate_weight, up_weight)

        mask_sib = send(tile_mask, sibling)
        job_mask = jnp.where(home, tile_mask, mask_sib).reshape(R, row_tiles * col_tiles)
        place = jnp.arange(row_tiles * col_tiles)
        upto = (place[None, :] <= place[:, None]).astype(jnp.int32)
        slot = jnp.sum(job_mask[:, None, :] * upto[None], axis=2) - 1
        codes = jnp.where(job_mask == 1, slot, -1).reshape(-1)

        crossed, tok_other = after(send(other, sibling), tok_other)
        keep = jnp.where(home, mine, crossed)
        give = jnp.where(home, crossed, mine)
        chunk_tiles = min(4, col_tiles)
        width = chunk_tiles * TILE

        def add_blocks(acc, todo, last=False):
            first = acc is None
            counts = tuple(len(values) for values, _ in todo)
            info = jnp.stack([block for _, block in todo] + [core]).astype(jnp.int32)
            acc_spec = pl.BlockSpec((2, rows, width), lambda g, *_: (0, 0, g))
            in_specs = [pl.BlockSpec((rows, depth), lambda g, codes, info, b=b: (0, info[b]))
                        for b in range(len(todo))]
            operands = [codes, info] + [tok] * len(todo)
            for values, _ in todo:
                operands += [v for v, _ in values] + [w for _, w in values]
            in_specs += [pl.BlockSpec(memory_space=pl.ANY)] * (2 * sum(counts))
            if not first:
                in_specs.append(acc_spec)
                operands.append(acc)
            if last:
                out_shape = jax.ShapeDtypeStruct((rows, cols), jnp.bfloat16)
                out_spec = pl.BlockSpec((rows, width), lambda g, *_: (0, g))
            else:
                out_shape = jax.ShapeDtypeStruct((2, rows, cols), jnp.float32)
                out_spec = acc_spec
            return pl.pallas_call(
                functools.partial(block_kernel, row_tiles, col_tiles, chunk_tiles, counts, first, last),
                out_shape=out_shape,
                grid_spec=pltpu.PrefetchScalarGridSpec(
                    num_scalar_prefetch=2,
                    grid=(cols // width,),
                    in_specs=in_specs,
                    out_specs=out_spec,
                    scratch_shapes=[pltpu.VMEM((len(todo), 2, slots, TILE, TILE), jnp.bfloat16),
                                    pltpu.VMEM((len(todo), 2, depth, width), jnp.bfloat16),
                                    pltpu.SemaphoreType.DMA((2 * sum(counts),))],
                ),
                input_output_aliases={} if first or last else {len(operands) - 1: 0},
                compiler_params=pltpu.CompilerParams(vmem_limit_bytes=VMEM_LIMIT),
                cost_estimate=pl.CostEstimate(
                    flops=rows * depth, bytes_accessed=rows * depth, transcendentals=0),
                name="block",
            )(*operands)

        def along(value, s):
            return send(value, lambda rr, cc: ((rr + 4 * s) % R, cc))

        def with_sibling(value):
            return (value, send(value, sibling))

        paired = send(give, z_pair)
        far = [along(keep, s) for s in range(1, NZ // 2)]
        tok_mine = jnp.where(home, tokens, tok_other)
        tok_sib = send(jnp.where(home, tok_other, tokens), sibling)
        wide = tokens.shape[1]
        both = jnp.where(core == 0, jnp.concatenate([tok_mine, tok_sib], 1),
                         jnp.concatenate([tok_sib, tok_mine], 1))
        y = lax.axis_index("col") // 2
        tok_parts = [send(both, lambda rr, cc, s=s: (rr, (cc + 2 * s) % C)) for s in range(1, C // 2)]
        keep_x = send(keep, x_pair)
        (tok_parts, keep_x), (far, paired) = after((tok_parts, keep_x), (far, paired))
        tok = jnp.zeros((rows, wide * C), tokens.dtype)
        tok = lax.dynamic_update_slice_in_dim(tok, both, y * 2 * wide, 1)
        for s, part in enumerate(tok_parts, 1):
            source = (y - s) % (C // 2)
            tok = lax.dynamic_update_slice_in_dim(tok, part, source * 2 * wide, 1)
        half = slots // 2
        acc = add_blocks(None, [([with_sibling(keep)], r), ([with_sibling(keep_x)], r ^ 1)])
        far_paired = [along(paired, s) for s in range(1, NZ // 2)]
        far_x = [send(value, x_pair) for value in far]
        paired_x = send(paired, x_pair)
        todo = [([with_sibling(paired)], r ^ 2)]
        for s, value in enumerate(far, 1):
            todo.append(([with_sibling(value)], (r - 4 * s) % R))
        for n in range(0, len(todo), 2):
            acc = add_blocks(acc, todo[n:n + 2])
        far_paired, acc = after(far_paired, acc)
        (far_x, paired_x), far_paired = after((far_x, paired_x), far_paired)
        last_a = [send(value[:half], x_pair) for value in far_paired]
        last_b = [along(paired_x[half:], s) for s in range(1, NZ // 2)]
        todo = [([with_sibling(paired_x)], r ^ 3)]
        for s, value in enumerate(far_x, 1):
            todo.append(([with_sibling(value)], ((r - 4 * s) % R) ^ 1))
        for s, value in enumerate(far_paired, 1):
            todo.append(([with_sibling(value)], ((r ^ 2) - 4 * s) % R))
        for n in range(0, len(todo), 2):
            acc = add_blocks(acc, todo[n:n + 2])
        (last_a, last_b), acc = after((last_a, last_b), acc)
        for s in range(1, NZ // 2):
            acc = add_blocks(acc, [([with_sibling(last_a[s - 1]), with_sibling(last_b[s - 1])],
                                    (((r ^ 2) - 4 * s) % R) ^ 1)], last=s == NZ // 2 - 1)
        return send(acc, swap_out)

    placed = (P("row", "col"), P("row", "col"), P("row", "col"), P(None, "col"))
    return jax.shard_map(
        on_device, mesh=mesh, in_specs=placed, out_specs=P("row", "col"), check_vma=False
    )
```

```python
import functools

import jax
import jax.numpy as jnp
from jax import lax
from jax.experimental import pallas as pl
from jax.experimental.pallas import tpu as pltpu
from jax.sharding import PartitionSpec as P

TILE = 128
VMEM_LIMIT = 56 * 1024 * 1024


def pack_kernel(row_tiles, col_tiles, core_ref, mask_ref, gate_ref, up_ref, mine_ref, other_ref):
    core = core_ref[0]

    def tile_step(i, j, slot):
        kept = mask_ref[i * col_tiles + j]
        rows = pl.ds(i * TILE, TILE)
        cols = pl.ds(pl.multiple_of(j * TILE, TILE), TILE)

        @pl.when((kept == 1) & (core == 0))
        def _():
            mine_ref[slot] = gate_ref[rows, cols]
            other_ref[slot] = up_ref[rows, cols]

        @pl.when((kept == 1) & (core == 1))
        def _():
            mine_ref[slot] = up_ref[rows, cols]
            other_ref[slot] = gate_ref[rows, cols]

        return slot + kept

    slot = jnp.int32(0)
    for i in range(row_tiles):
        slot = lax.fori_loop(0, col_tiles, functools.partial(tile_step, i), slot)


def block_kernel(row_tiles, col_tiles, chunk_tiles, counts, first, last, codes_ref, info_ref, *rest):
    blocks = len(counts)
    tok_refs, rest = rest[:blocks], rest[blocks:]
    pieces, rest = rest[:2 * sum(counts)], rest[2 * sum(counts):]
    if first:
        acc_ref = None
    else:
        acc_ref, rest = rest[0], rest[1:]
    out_ref, packed, dense, sems = rest
    core = info_ref[blocks]
    chunk = pl.program_id(0)

    @pl.when(chunk == 0)
    def _():
        copies = []
        for b in range(blocks):
            for kind in range(2):
                start = 0
                for _ in range(counts[b]):
                    ref = pieces[len(copies)]
                    copies.append(pltpu.make_async_copy(
                        ref, packed.at[b, kind, pl.ds(start, ref.shape[0])], sems.at[len(copies)]))
                    start += ref.shape[0]
        for copy in copies:
            copy.start()
        for copy in copies:
            copy.wait()

    sums = []
    for kind in range(2):
        total = None if first else acc_ref[kind]
        for b in range(blocks):
            for i in range(row_tiles):
                for j in range(chunk_tiles):
                    code = codes_ref[(info_ref[b] * row_tiles + i) * col_tiles + chunk * chunk_tiles + j]
                    tile = packed[b, kind, jnp.maximum(code, 0)]
                    dense[b, kind, pl.ds(i * TILE, TILE), pl.ds(j * TILE, TILE)] = jnp.where(
                        code >= 0, tile, jnp.zeros_like(tile))
            product = jnp.dot(tok_refs[b][...], dense[b, kind], preferred_element_type=jnp.float32)
            total = product if total is None else total + product
        if last:
            sums.append(total)
        else:
            out_ref[kind] = total
    if last:
        gate = jnp.where(core == 0, sums[0], sums[1])
        up = jnp.where(core == 0, sums[1], sums[0])
        out_ref[...] = (gate / (1.0 + jnp.exp(-gate)) * up).astype(out_ref.dtype)


def solution(mesh):
    R, C = mesh.shape["row"], mesh.shape["col"]
    NZ = R // 2
    axes = ("row", "col")

    def send(value, move):
        pairs = []
        for r in range(R):
            for c in range(C):
                tr, tc = move(r, c)
                pairs.append((r * C + c, tr * C + tc))
        return lax.ppermute(value, axes, pairs)

    sibling = lambda r, c: (r, c ^ 1)
    z_pair = lambda r, c: (r ^ 2, c)
    x_pair = lambda r, c: (r ^ 1, c)

    def swap_out(r, c):
        return (r, c) if ((r // 2) % 2) == (c % 2) else (r ^ 2, c ^ 1)

    def on_device(tokens, gate_weight, up_weight, tile_mask):
        depth, cols = gate_weight.shape
        row_tiles, col_tiles = depth // TILE, cols // TILE
        slots = 5 * row_tiles * col_tiles // 8
        rows = tokens.shape[0]
        r = lax.axis_index("row")
        core = lax.axis_index("col") % 2
        home = ((r // 2) % 2) == core

        def after(value, acc):
            return lax.optimization_barrier((value, acc))

        tok_other = send(tokens, z_pair)
        smem = pl.BlockSpec(memory_space=pltpu.SMEM)
        vmem = pl.BlockSpec(memory_space=pltpu.VMEM)
        own_mask = lax.dynamic_slice_in_dim(tile_mask, r * row_tiles, row_tiles, 0).reshape(-1)
        piece = jax.ShapeDtypeStruct((slots, TILE, TILE), gate_weight.dtype)
        mine, other = pl.pallas_call(
            functools.partial(pack_kernel, row_tiles, col_tiles),
            out_shape=(piece, piece),
            in_specs=[smem, smem, vmem, vmem],
            out_specs=(vmem, vmem),
            compiler_params=pltpu.CompilerParams(vmem_limit_bytes=VMEM_LIMIT),
            name="pack",
        )(core.reshape(1).astype(jnp.int32), own_mask, gate_weight, up_weight)

        mask_sib = send(tile_mask, sibling)
        job_mask = jnp.where(home, tile_mask, mask_sib).reshape(R, row_tiles * col_tiles)
        place = jnp.arange(row_tiles * col_tiles)
        upto = (place[None, :] <= place[:, None]).astype(jnp.int32)
        slot = jnp.sum(job_mask[:, None, :] * upto[None], axis=2) - 1
        codes = jnp.where(job_mask == 1, slot, -1).reshape(-1)

        crossed, tok_other = after(send(other, sibling), tok_other)
        keep = jnp.where(home, mine, crossed)
        give = jnp.where(home, crossed, mine)
        chunk_tiles = min(4, col_tiles)
        width = chunk_tiles * TILE

        def add_blocks(acc, todo, last=False):
            first = acc is None
            counts = tuple(len(values) for values, _ in todo)
            info = jnp.stack([block for _, block in todo] + [core]).astype(jnp.int32)
            acc_spec = pl.BlockSpec((2, rows, width), lambda g, *_: (0, 0, g))
            in_specs = [pl.BlockSpec((rows, depth), lambda g, codes, info, b=b: (0, info[b]))
                        for b in range(len(todo))]
            operands = [codes, info] + [tok] * len(todo)
            for values, _ in todo:
                operands += [v for v, _ in values] + [w for _, w in values]
            in_specs += [pl.BlockSpec(memory_space=pl.ANY)] * (2 * sum(counts))
            if not first:
                in_specs.append(acc_spec)
                operands.append(acc)
            if last:
                out_shape = jax.ShapeDtypeStruct((rows, cols), jnp.bfloat16)
                out_spec = pl.BlockSpec((rows, width), lambda g, *_: (0, g))
            else:
                out_shape = jax.ShapeDtypeStruct((2, rows, cols), jnp.float32)
                out_spec = acc_spec
            return pl.pallas_call(
                functools.partial(block_kernel, row_tiles, col_tiles, chunk_tiles, counts, first, last),
                out_shape=out_shape,
                grid_spec=pltpu.PrefetchScalarGridSpec(
                    num_scalar_prefetch=2,
                    grid=(cols // width,),
                    in_specs=in_specs,
                    out_specs=out_spec,
                    scratch_shapes=[pltpu.VMEM((len(todo), 2, slots, TILE, TILE), jnp.bfloat16),
                                    pltpu.VMEM((len(todo), 2, depth, width), jnp.bfloat16),
                                    pltpu.SemaphoreType.DMA((2 * sum(counts),))],
                ),
                input_output_aliases={} if first or last else {len(operands) - 1: 0},
                compiler_params=pltpu.CompilerParams(vmem_limit_bytes=VMEM_LIMIT),
                cost_estimate=pl.CostEstimate(
                    flops=rows * depth, bytes_accessed=rows * depth, transcendentals=0),
                name="block",
            )(*operands)

        def along(value, s):
            return send(value, lambda rr, cc: ((rr + 4 * s) % R, cc))

        def with_sibling(value):
            return (value, send(value, sibling))

        paired = send(give, z_pair)
        far = [along(keep, s) for s in range(1, NZ // 2)]
        tok_mine = jnp.where(home, tokens, tok_other)
        tok_sib = send(jnp.where(home, tok_other, tokens), sibling)
        wide = tokens.shape[1]
        both = jnp.where(core == 0, jnp.concatenate([tok_mine, tok_sib], 1),
                         jnp.concatenate([tok_sib, tok_mine], 1))
        y = lax.axis_index("col") // 2
        tok_parts = [send(both, lambda rr, cc, s=s: (rr, (cc + 2 * s) % C)) for s in range(1, C // 2)]
        keep_x = send(keep, x_pair)
        (tok_parts, keep_x), (far, paired) = after((tok_parts, keep_x), (far, paired))
        tok = jnp.zeros((rows, wide * C), tokens.dtype)
        tok = lax.dynamic_update_slice_in_dim(tok, both, y * 2 * wide, 1)
        for s, part in enumerate(tok_parts, 1):
            source = (y - s) % (C // 2)
            tok = lax.dynamic_update_slice_in_dim(tok, part, source * 2 * wide, 1)
        half = 2 * slots // 3
        acc = add_blocks(None, [([with_sibling(keep)], r), ([with_sibling(keep_x)], r ^ 1)])
        far_paired = [along(paired, s) for s in range(1, NZ // 2)]
        far_x = [send(value, x_pair) for value in far]
        paired_x = send(paired, x_pair)
        todo = [([with_sibling(paired)], r ^ 2)]
        for s, value in enumerate(far, 1):
            todo.append(([with_sibling(value)], (r - 4 * s) % R))
        for n in range(0, len(todo), 2):
            acc = add_blocks(acc, todo[n:n + 2])
        far_paired, acc = after(far_paired, acc)
        (far_x, paired_x), far_paired = after((far_x, paired_x), far_paired)
        last_a = [send(value[:half], x_pair) for value in far_paired]
        last_b = [along(paired_x[half:], s) for s in range(1, NZ // 2)]
        todo = [([with_sibling(paired_x)], r ^ 3)]
        for s, value in enumerate(far_x, 1):
            todo.append(([with_sibling(value)], ((r - 4 * s) % R) ^ 1))
        for s, value in enumerate(far_paired, 1):
            todo.append(([with_sibling(value)], ((r ^ 2) - 4 * s) % R))
        for n in range(0, len(todo), 2):
            acc = add_blocks(acc, todo[n:n + 2])
        (last_a, last_b), acc = after((last_a, last_b), acc)
        for s in range(1, NZ // 2):
            acc = add_blocks(acc, [([with_sibling(last_a[s - 1]), with_sibling(last_b[s - 1])],
                                    (((r ^ 2) - 4 * s) % R) ^ 1)], last=s == NZ // 2 - 1)
        return send(acc, swap_out)

    placed = (P("row", "col"), P("row", "col"), P("row", "col"), P(None, "col"))
    return jax.shard_map(
        on_device, mesh=mesh, in_specs=placed, out_specs=P("row", "col"), check_vma=False
    )
```
